256 devices in a mesh: station: 64 (over x, z_lo, y, core), window: 4 (over z_hi).
Axes of the slice: x: 4, y: 4, z: 8 (z_hi: 4, z_lo: 2; z = z_hi * 2 + z_lo), core: 2. Of those that a mesh axis runs over, the one named last changes fastest.
Arguments:
- spectra: bfloat16 [256, 24, 3, 2, 4608], P('station', 'window'), may hold values from -6 to 6
- valid_mask: int32 [256, 24], P('station', 'window'), may hold values 0 or 1
- plan: int32 [2], replicated, may hold values from 0 to 63
Outputs:
- stacks: float32 [4, 2, 3, 256, 3, 512], P('window', None, None, 'station')
The draws below stay inside these ranges and needn't reach their ends.
Inputs may be any that keep to these rules, and one draw needn't show every extreme that they name: `plan`: each entry is a station block index.
All inputs are finite; a program needn't handle non-finite values. No bound on the sum of `valid_mask` on one device may be relied on, other than what follows from the above.
Results may differ from the reference program's by a relative error of at most 0.0003.
Values may be sent and summed in bfloat16 or wider, within the bound.
No kernel may reach another device: no remote copies, remote signals or barrier semaphores. Data moves between devices by JAX's collectives and lax.ppermute only.
A program may use at most 128 MiB of HBM per device.

```python
import math
import jax
import jax.numpy as jnp
from jax import lax

SB = 4
NF = 4608
LAGS = 512
NW = 18000
STEPS = 2
STATIONS = 256
HOURS = 24
N_STATION = 64


def touch_ends(values, rng, smallest, largest):
    spot = [jax.random.randint(jax.random.fold_in(rng, axis), (), 0, length) for axis, length in enumerate(values.shape)]
    longest = values.shape.index(max(values.shape))
    beside = spot[:longest] + [(spot[longest] + 1) % values.shape[longest]] + spot[longest + 1:]
    return values.at[tuple(spot)].set(smallest).at[tuple(beside)].set(largest)


def shard_levels(stream_key, extent, split, least, high):
    def one(dim, shards_of):
        draws = jax.random.uniform(jax.random.fold_in(jax.random.fold_in(stream_key, 6), dim), (shards_of,), jnp.float32, least / len(split), high / len(split))
        return jnp.repeat(jnp.exp(draws), extent[dim] // shards_of).reshape((-1,) + (1,) * (len(extent) - dim - 1))

    level = one(*split[0])
    for cut in split[1:]:
        level = level * one(*cut)
    return level


def centred(own_key, shape, scale, most, shards=(), kind=jnp.bfloat16):
    array = jax.random.normal(own_key, shape, jnp.float32) * scale
    if len(shards) > 0:
        array = shard_levels(own_key, shape, shards, -0.22, 0.18) * array
    return jnp.clip(array, min=-most, max=most).astype(kind)


def setup_inputs(seed: int = 0) -> dict:
    keys = jax.random.split(jax.random.key(seed), 4)
    spectra = centred(keys[0], (STATIONS, HOURS, 3, 2, NF), 1.0, 6.0, ((0, 64), (1, 4)))
    valid_mask = touch_ends((jax.random.randint(keys[1], (STATIONS, HOURS), 0, 6) < 5).astype(jnp.int32), jax.random.fold_in(keys[1], 1), 0, 1)
    plan = jax.random.randint(keys[2], (STEPS,), 0, N_STATION).astype(jnp.int32)
    return {"spectra": spectra, "valid_mask": valid_mask, "plan": plan}


def make_basis(bins, lag_count, samples, hours):
    freqs = jnp.arange(bins, dtype=jnp.int32)[:, None]
    shifts = jnp.arange(lag_count, dtype=jnp.int32)[None, :] - lag_count // 2
    phases = jnp.mod(freqs * shifts, samples)
    angles = phases.astype(jnp.float32) * (2.0 * math.pi / samples)
    factor = 1.0 / math.sqrt(2.0 * bins * hours)
    return jnp.concatenate([jnp.cos(angles), -jnp.sin(angles)], 0) * factor

def cross_spectra(left, right):
    left_count = left.shape[0]
    right_count = right.shape[0]
    bins = left.shape[-1]
    empty = jnp.zeros((left_count, 3, right_count, 3, bins), jnp.float32)

    def add_hour(hour, totals):
        left_hour = lax.dynamic_index_in_dim(left, hour, 1, keepdims=False).astype(jnp.float32)
        right_hour = lax.dynamic_index_in_dim(right, hour, 1, keepdims=False).astype(jnp.float32)
        left_re = left_hour[:, :, 0][:, :, None, None, :]
        left_im = left_hour[:, :, 1][:, :, None, None, :]
        right_re = right_hour[:, :, 0][None, None, :, :, :]
        right_im = right_hour[:, :, 1][None, None, :, :, :]
        real_part = totals[0] + (left_re * right_re + left_im * right_im)
        imag_part = totals[1] + (left_re * right_im - left_im * right_re)
        return (real_part, imag_part)
    return lax.fori_loop(0, left.shape[1], add_hour, (empty, empty))

def inverse_lags(real_part, imag_part, lag_basis):
    joined = jnp.concatenate([real_part, imag_part], -1)
    shape = joined.shape
    result = jnp.dot(joined.reshape(-1, shape[-1]), lag_basis, precision=lax.Precision.HIGHEST, preferred_element_type=jnp.float32)
    return result.reshape(shape[:-1] + (lag_basis.shape[1],))

def reference(spectra, valid_mask, plan):
    masked = spectra * valid_mask.astype(jnp.bfloat16)[:, :, None, None, None]
    lag_basis = make_basis(NF, LAGS, NW, HOURS)
    blocks = masked.reshape((N_STATION, SB) + masked.shape[1:])
    results = []
    for which_step in range(STEPS):
        first_row = (plan[which_step] * SB).astype(jnp.int32)
        owner_rows = lax.dynamic_slice_in_dim(masked, first_row, SB, 0)

        def one_block(block):
            real_part, imag_part = cross_spectra(owner_rows, block)
            return inverse_lags(real_part, imag_part, lag_basis)
        per_block = lax.map(one_block, blocks)
        arranged = jnp.transpose(per_block, (1, 2, 0, 3, 4, 5)).reshape(SB, 3, STATIONS, 3, LAGS)
        results.append(arranged)
    return jnp.stack(results, 1)
```

```python
import functools
import math

import jax
import jax.numpy as jnp
import ml_dtypes
import numpy as np
from jax import lax
from jax.experimental import pallas as pl
from jax.experimental.pallas import tpu as pltpu
from jax.sharding import PartitionSpec as P

LAGS = 512
NW = 18000
STEPS = 2
HALF = LAGS // 2
LANES = 128
CORES = 2
WAYS = 4
DEPTH = 256


def tables(bins, hours):
    freqs = np.arange(bins, dtype=np.int64)[:, None]
    odd = 2 * np.arange(HALF, dtype=np.int64)[None, :] + 1
    angles = ((freqs * odd) % (2 * NW)).astype(np.float64) * (math.pi / NW)
    factor = 1.0 / math.sqrt(2.0 * bins * hours)
    parts = []
    for table in (np.cos(angles) * factor, np.sin(angles) * factor):
        head = table.astype(ml_dtypes.bfloat16)
        tail = (table - head.astype(np.float64)).astype(ml_dtypes.bfloat16)
        parts += [head, tail]
    basis = np.stack(parts, 0)
    turn = np.arange(bins, dtype=np.float64) * (math.pi / NW)
    turns = np.stack([np.cos(turn), np.sin(turn)], 0).astype(np.float32)
    turns = turns.reshape(2, bins // LANES, LANES).transpose(1, 0, 2)
    return basis, np.ascontiguousarray(turns)


def coords(index):
    return (index >> 4) & 3, (index >> 3) & 1, (index >> 1) & 3, index & 1


def pair_permute(value, shift):
    size = lax.axis_size("station")
    return lax.ppermute(value, "station", [(s, s ^ shift) for s in range(size)])


def along_x(value, distance):
    return pair_permute(value, distance << 4)


def along_y(value, distance):
    return pair_permute(value, distance << 1)


def pick(which, values):
    result = values[-1]
    for number in range(len(values) - 2, -1, -1):
        result = jnp.where(which == number, values[number], result)
    return result


def correlate_kernel(place, q0, q1, q2, q3, own, other, turns, basis, mine, theirs,
                     owner, local, lefts, acc):
    chunk = pl.program_id(0)
    last = pl.num_programs(0) - 1
    rows = own.shape[1]
    sub = rows // WAYS
    tiles = turns.shape[0]
    hours = 6
    first, second, window = place[0], place[1], place[2]

    def cross(which, slot):
        for part in range(2):
            tile = which * 2 + part
            lanes = slice(part * LANES, (part + 1) * LANES)
            turn = turns[tile]
            turn_re = jnp.broadcast_to(turn[0:1], (8, LANES))
            turn_im = jnp.broadcast_to(turn[1:2], (8, LANES))
            right = []
            for hour in range(hours):
                for comp in range(3):
                    at = (hour * 3 + comp) * 2 * tiles + tile * 2
                    x_re = local[pl.ds(at, 8, stride=rows), :]
                    x_im = local[pl.ds(at + 1, 8, stride=rows), :]
                    right.append((x_re * turn_re + x_im * turn_im, x_im * turn_re - x_re * turn_im))
            done = []
            for slot_i in range(WAYS):
                base = (window ^ slot_i) * rows + tile * 2
                for comp_i in range(3):
                    re = [None] * 3
                    im = [None] * 3
                    for hour in range(hours):
                        at = base + (hour * 3 + comp_i) * 2 * tiles
                        o_re = jnp.broadcast_to(owner[pl.ds(at, 1), :], (8, LANES))
                        o_im = jnp.broadcast_to(owner[pl.ds(at + 1, 1), :], (8, LANES))
                        for comp in range(3):
                            x_re, x_im = right[hour * 3 + comp]
                            new_re = o_re * x_re + o_im * x_im
                            new_im = o_re * x_im - o_im * x_re
                            re[comp] = new_re if hour == 0 else re[comp] + new_re
                            im[comp] = new_im if hour == 0 else im[comp] + new_im
                    done.append((re, im))
                    if len(done) == 2:
                        number = slot_i * 3 + comp_i - 1
                        where = slice(number * 24, number * 24 + 48)
                        for kind in range(2):
                            value = jnp.concatenate(done[0][kind] + done[1][kind], 0)
                            head = value.astype(jnp.bfloat16)
                            tail = (value - head.astype(jnp.float32)).astype(jnp.bfloat16)
                            lefts[slot, 2 * kind, where, lanes] = head
                            lefts[slot, 2 * kind + 1, where, lanes] = tail
                        done = []

    def transform(slot):
        for kind in range(2):
            head = lefts[slot, 2 * kind]
            tail = lefts[slot, 2 * kind + 1]
            table = basis[2 * kind]
            rest = basis[2 * kind + 1]
            dot = functools.partial(jnp.dot, preferred_element_type=jnp.float32)
            acc[kind] += dot(head, table) + dot(tail, table) + dot(head, rest)

    @pl.when(chunk == 0)
    def _():
        acc[...] = jnp.zeros_like(acc)
        for near, piece in enumerate((q0, q1, q2, q3)):
            base = (first ^ near) * rows
            for step in range(WAYS):
                at = pl.multiple_of(base + (second ^ step) * sub, 8)
                owner[pl.ds(at, sub), :] = piece[step].astype(jnp.float32)
        for near, source in enumerate((own, other)):
            for station in range(WAYS):
                at = (near * WAYS + station) * rows
                local[at:at + rows, :] = source[station].astype(jnp.float32)
        cross(0, 0)

    @pl.when(chunk < last)
    def _():
        cross(chunk + 1, lax.rem(chunk + 1, 2))
        transform(lax.rem(chunk, 2))

    @pl.when(chunk == last)
    def _():
        transform(lax.rem(chunk, 2))
        for kind in range(2):
            lanes = slice(kind * HALF, (kind + 1) * HALF)
            total = acc[kind].reshape(36, 8, HALF)
            mine[:, :, lanes] = total[:, 0:4]
            theirs[:, :, lanes] = total[:, 4:8]


def correlate(place, pieces, own, other, turns, basis):
    rows = own.shape[1]
    tiles = turns.shape[0] // CORES
    chunks = tiles * LANES // DEPTH

    def whole(shape):
        return pl.BlockSpec(shape, lambda k, s: (0,) * len(shape))

    spec = pltpu.PrefetchScalarGridSpec(
        num_scalar_prefetch=1,
        grid=(chunks,),
        in_specs=[whole(p.shape) for p in pieces]
        + [whole(own.shape), whole(other.shape)]
        + [pl.BlockSpec((tiles, 2, LANES), lambda k, s: (s[3], 0, 0)),
           pl.BlockSpec((4, DEPTH, HALF), lambda k, s: (0, s[3] * chunks + k, 0))],
        out_specs=[whole((36, 4, LAGS)), whole((36, 4, LAGS))],
        scratch_shapes=[
            pltpu.VMEM((WAYS * rows, LANES), jnp.float32),
            pltpu.VMEM((CORES * WAYS * rows, LANES), jnp.float32),
            pltpu.VMEM((2, 4, 288, DEPTH), jnp.bfloat16),
            pltpu.VMEM((2, 288, HALF), jnp.float32),
        ],
    )
    out = jax.ShapeDtypeStruct((36, 4, LAGS), jnp.float32)
    return pl.pallas_call(
        correlate_kernel,
        grid_spec=spec,
        out_shape=[out, out],
        compiler_params=pltpu.CompilerParams(vmem_limit_bytes=40 * 2**20),
        cost_estimate=pl.CostEstimate(flops=8 * 10**9, bytes_accessed=10**7, transcendentals=0),
    )(place, *pieces, own, other, turns, basis)


def finish_kernel(a0, a1, a2, a3, b0, b1, b2, b3, flip, out):
    for step, parts in enumerate(((a0, a1, a2, a3), (b0, b1, b2, b3))):
        total = (parts[0][...] + parts[1][...]) + (parts[2][...] + parts[3][...])
        even = total[:, :, 0:HALF]
        odd = total[:, :, HALF:LAGS]
        early = (even + odd).reshape(36, HALF)
        early = jnp.dot(early, flip[...], precision=lax.Precision.HIGHEST,
                        preferred_element_type=jnp.float32).reshape(9, 4, HALF)
        late = even - odd
        for a in range(3):
            for b in range(3):
                out[0, step, a, :, b, 0:HALF] = early[a * 3 + b]
                out[0, step, a, :, b, HALF:LAGS] = late[a * 3 + b]


def finish(parts, flip):
    return pl.pallas_call(
        finish_kernel,
        out_shape=jax.ShapeDtypeStruct((1, STEPS, 3, 4, 3, LAGS), jnp.float32),
        compiler_params=pltpu.CompilerParams(vmem_limit_bytes=16 * 2**20),
    )(*parts[0], *parts[1], flip)


def body(spectra, valid_mask, plan):
    windows = lax.axis_size("window")
    stations, hours, comps, _, bins = spectra.shape
    tiles = bins // LANES
    half = tiles // CORES
    used = hours * comps * half * 2
    rows = -(-used // 32) * 32
    x, z, y, core = coords(lax.axis_index("station"))
    window = lax.axis_index("window")

    masked = spectra * valid_mask.astype(jnp.bfloat16)[:, :, None, None, None]
    masked = masked.reshape(stations, hours * comps, 2, tiles, LANES).transpose(0, 1, 3, 2, 4)
    halves = []
    for number in range(CORES):
        piece = masked[:, :, number * half:(number + 1) * half].reshape(stations, used, LANES)
        halves.append(jnp.pad(piece, ((0, 0), (0, rows - used), (0, 0))))
    own = jnp.where(core == 0, halves[0], halves[1])
    other = pair_permute(jnp.where(core == 0, halves[1], halves[0]), 1)

    sub = rows // WAYS
    moves = ((along_x, along_y), (along_y, along_x))
    places = []
    small = []
    for step in range(STEPS):
        root_x, root_z, root_y, root_core = coords(plan[step])
        near_x, near_y = root_x ^ x, root_y ^ y
        first, second = ((near_x, near_y), (near_y, near_x))[step]
        go_first, go_second = moves[step]
        block = jnp.where(root_core == core, own, other)
        parts = [block[0]] + [go_first(block[d], d) for d in range(1, WAYS)]
        piece = pick(first, parts).reshape(WAYS, sub, LANES)
        parts = [piece[0]] + [go_second(piece[d], d) for d in range(1, WAYS)]
        small.append(pick(second, parts))
        places.append((first, second, root_z == z))
    both = jnp.stack(small, 0)
    across = pair_permute(both, 8)
    totals = []
    basis, turns = tables(bins, hours * windows)
    for step in range(STEPS):
        first, second, here = places[step]
        go_first, go_second = moves[step]
        mine = jnp.where(here, both[step], across[step])
        piece = jnp.stack([mine] + [go_second(mine, d) for d in range(1, WAYS)], 0)
        pieces = [piece] + [go_first(piece, d) for d in range(1, WAYS)]
        place = jnp.stack([first, second, window, core]).astype(jnp.int32)
        kept, given = correlate(place, pieces, own, other, jnp.asarray(turns), jnp.asarray(basis))
        total = (kept + pair_permute(given, 1)).reshape(windows, 9, 4, LAGS)
        totals.append([total[0]] + [
            lax.ppermute(total[d], "window", [(w, w ^ d) for w in range(windows)])
            for d in range(1, windows)])
    flip = jnp.asarray(np.eye(HALF, dtype=np.float32)[::-1].copy())
    return finish(totals, flip)


def solution(mesh):
    return jax.shard_map(
        body,
        mesh=mesh,
        in_specs=(P("station", "window", None, None, None), P("station", "window"), P()),
        out_specs=P("window", None, None, "station", None, None),
        check_vma=False,
    )
```

```python
import functools
import math

import jax
import jax.numpy as jnp
import ml_dtypes
import numpy as np
from jax import lax
from jax.experimental import pallas as pl
from jax.experimental.pallas import tpu as pltpu
from jax.sharding import PartitionSpec as P

LAGS = 512
NW = 18000
STEPS = 2
HALF = LAGS // 2
LANES = 128
CORES = 2
WAYS = 4
DEPTH = 256


def tables(bins, hours):
    freqs = np.arange(bins, dtype=np.int64)[:, None]
    odd = 2 * np.arange(HALF, dtype=np.int64)[None, :] + 1
    angles = ((freqs * odd) % (2 * NW)).astype(np.float64) * (math.pi / NW)
    factor = 1.0 / math.sqrt(2.0 * bins * hours)
    parts = []
    for table in (np.cos(angles) * factor, np.sin(angles) * factor):
        head = table.astype(ml_dtypes.bfloat16)
        tail = (table - head.astype(np.float64)).astype(ml_dtypes.bfloat16)
        parts += [head, tail]
    basis = np.stack(parts, 0).reshape(2, 2, CORES, -1, DEPTH, HALF)
    basis = np.ascontiguousarray(basis.transpose(2, 3, 0, 1, 4, 5))
    turn = np.arange(bins, dtype=np.float64) * (math.pi / NW)
    turns = np.stack([np.cos(turn), np.sin(turn)], 0).astype(np.float32)
    turns = turns.reshape(2, CORES, bins // LANES // CORES, LANES).transpose(1, 2, 0, 3)
    return basis, np.ascontiguousarray(turns)


def coords(index):
    return (index >> 4) & 3, (index >> 3) & 1, (index >> 1) & 3, index & 1


def pair_permute(value, even, odd=None):
    size = lax.axis_size("station")
    shifts = (even, even if odd is None else odd)
    return lax.ppermute(value, "station", [(s, s ^ shifts[s & 1]) for s in range(size)])


def along_first(value, distance):
    return pair_permute(value, distance << 4, distance << 1)


def along_second(value, distance):
    return pair_permute(value, distance << 1, distance << 4)


def pick(which, values):
    result = values[-1]
    for number in range(len(values) - 2, -1, -1):
        result = jnp.where(which == number, values[number], result)
    return result


def turn_kernel(own, other, turns, out, local):
    rows = own.shape[1]
    tiles = out.shape[0]
    for near, source in enumerate((own, other)):
        for station in range(WAYS):
            at = (near * WAYS + station) * rows
            local[at:at + rows, :] = source[station].astype(jnp.float32)

    def one(tile, carry):
        turn = turns[tile]
        turn_re = jnp.broadcast_to(turn[0:1], (8, LANES))
        turn_im = jnp.broadcast_to(turn[1:2], (8, LANES))
        for part in range(18):
            at = part * 2 * tiles + tile * 2
            x_re = local[pl.ds(at, 8, stride=rows), :]
            x_im = local[pl.ds(at + 1, 8, stride=rows), :]
            out[tile, 2 * part] = x_re * turn_re + x_im * turn_im
            out[tile, 2 * part + 1] = x_im * turn_re - x_re * turn_im
        return carry

    lax.fori_loop(0, tiles, one, 0)


def turn_right(own, other, turns):
    tiles = turns.shape[0]
    rows = own.shape[1]
    return pl.pallas_call(
        turn_kernel,
        in_specs=[pl.BlockSpec(memory_space=pltpu.VMEM)] * 3,
        out_specs=pl.BlockSpec(memory_space=pltpu.VMEM),
        out_shape=jax.ShapeDtypeStruct((tiles, 36, 8, LANES), jnp.float32),
        scratch_shapes=[pltpu.VMEM((8 * rows, LANES), jnp.float32)],
        compiler_params=pltpu.CompilerParams(vmem_limit_bytes=16 * 2**20),
        cost_estimate=pl.CostEstimate(flops=10**7, bytes_accessed=10**6, transcendentals=0),
    )(own, other, turns)


def correlate_kernel(slots, place, own, other, right, basis,
                     mine, theirs, owner, lefts, acc, tables, sems):
    rows = own.shape[1]
    sub = rows // WAYS
    tiles = right.shape[0]
    chunks = tiles * LANES // DEPTH
    window, core = place[2], place[3]
    size = WAYS * rows

    def bring(chunk):
        return pltpu.make_async_copy(basis.at[core, chunk], tables.at[chunk], sems.at[chunk])

    for chunk in range(chunks):
        bring(chunk).start()

    def cross(chunk, slot):
        for part in range(2):
            tile = chunk * 2 + part
            lanes = part * LANES
            turned = [right[tile, n] for n in range(36)]
            sums = [turned[2 * n] + turned[2 * n + 1] for n in range(18)]
            done = []
            for number in range(STEPS * len(slots) * 3):
                step, rest = divmod(number, len(slots) * 3)
                slot_i, comp_i = divmod(rest, 3)
                start = step * size + (window ^ slots[slot_i]) * rows + tile * 2
                parts = [None] * 3
                for hour in range(6):
                    at = start + (hour * 3 + comp_i) * 2 * tiles
                    o_re = jnp.broadcast_to(owner[pl.ds(at, 1), :], (8, LANES))
                    o_im = jnp.broadcast_to(owner[pl.ds(at + 1, 1), :], (8, LANES))
                    o_sum = o_re + o_im
                    o_dif = o_re - o_im
                    for comp in range(3):
                        at = hour * 3 + comp
                        new = (o_re * sums[at], o_sum * turned[2 * at], o_dif * turned[2 * at + 1])
                        parts[comp] = new if hour == 0 else [p + n for p, n in zip(parts[comp], new)]
                done.append(([p[0] - p[2] for p in parts], [p[0] - p[1] for p in parts]))
                if len(done) == 2:
                    where = slice((number - 1) * 24, (number + 1) * 24)
                    for kind in range(2):
                        value = jnp.concatenate(done[0][kind] + done[1][kind], 0)
                        head = value.astype(jnp.bfloat16)
                        tail = (value - head.astype(jnp.float32)).astype(jnp.bfloat16)
                        lefts[slot, kind, where, lanes:lanes + LANES] = head
                        lefts[slot, kind, where, DEPTH + lanes:DEPTH + lanes + LANES] = tail
                    done = []

    def transform(chunk, slot):
        dot = functools.partial(jnp.dot, preferred_element_type=jnp.float32)
        for kind in range(2):
            head = lefts[slot, kind, :, 0:DEPTH]
            tail = lefts[slot, kind, :, DEPTH:2 * DEPTH]
            table = tables[chunk, kind, 0]
            rest = tables[chunk, kind, 1]
            acc[kind] += dot(head, table) + dot(tail, table) + dot(head, rest)

    acc[...] = jnp.zeros_like(acc)
    for step, pieces in ((core, own), (1 - core, other)):
        first, second = place[4 * step], place[4 * step + 1]
        for near in range(WAYS):
            piece = pieces[near].astype(jnp.float32)
            for number in range(WAYS):
                at = pl.multiple_of(step * size + (first ^ near) * rows + (second ^ number) * sub, 8)
                owner[pl.ds(at, sub), :] = piece[number * sub:(number + 1) * sub]
    cross(0, 0)

    def one(chunk, carry):
        slot = lax.rem(chunk, 2)
        bring(chunk).wait()
        transform(chunk, slot)
        cross(chunk + 1, 1 - slot)
        return carry

    lax.fori_loop(0, chunks - 1, one, 0)
    slot = (chunks - 1) % 2
    bring(chunks - 1).wait()
    transform(chunks - 1, slot)
    for kind in range(2):
        lanes = slice(kind * HALF, (kind + 1) * HALF)
        total = acc[kind].reshape(STEPS, len(slots), 9, 8, HALF)
        for step in range(STEPS):
            here = slice(step * 9, step * 9 + 9)
            mine[:, here, :, lanes] = total[step, :, :, 0:4]
            theirs[:, here, :, lanes] = total[step, :, :, 4:8]


def correlate(slots, place, own, other, right, basis):
    rows = own.shape[1]
    chunks = basis.shape[1]
    lines = STEPS * len(slots) * 72
    out = jax.ShapeDtypeStruct((len(slots), STEPS * 9, 4, LAGS), jnp.float32)
    return pl.pallas_call(
        functools.partial(correlate_kernel, slots),
        in_specs=[pl.BlockSpec(memory_space=pltpu.SMEM)]
        + [pl.BlockSpec(memory_space=pltpu.VMEM)] * 3
        + [pl.BlockSpec(memory_space=pl.ANY)],
        out_specs=[pl.BlockSpec(memory_space=pltpu.VMEM)] * 2,
        out_shape=[out, out],
        scratch_shapes=[
            pltpu.VMEM((STEPS * WAYS * rows, LANES), jnp.float32),
            pltpu.VMEM((2, 2, lines, 2 * DEPTH), jnp.bfloat16),
            pltpu.VMEM((2, lines, HALF), jnp.float32),
            pltpu.VMEM(basis.shape[1:], jnp.bfloat16),
            pltpu.SemaphoreType.DMA((chunks,)),
        ],
        compiler_params=pltpu.CompilerParams(vmem_limit_bytes=50 * 2**20),
        cost_estimate=pl.CostEstimate(flops=lines * 3 * 10**7, bytes_accessed=10**6, transcendentals=0),
    )(place, own, other, right, basis)


def finish_kernel(m0, t0, p1, p2, p3, flip, out):
    total = (m0[0] + t0[0]) + (p1[...] + (p2[...] + p3[...]))
    even = total[:, :, 0:HALF]
    odd = total[:, :, HALF:LAGS]
    early = jnp.dot((even + odd).reshape(72, HALF), flip[...], precision=lax.Precision.HIGHEST,
                    preferred_element_type=jnp.float32)
    out[0, :, :, :, :, 0:HALF] = early.reshape(STEPS, 3, 3, 4, HALF)
    out[0, :, :, :, :, HALF:LAGS] = (even - odd).reshape(STEPS, 3, 3, 4, HALF)


def finish(parts, flip):
    return pl.pallas_call(
        finish_kernel,
        out_shape=jax.ShapeDtypeStruct((1, STEPS, 3, 3, 4, LAGS), jnp.float32),
        compiler_params=pltpu.CompilerParams(vmem_limit_bytes=16 * 2**20),
    )(*parts, flip)


def pad_rows(value, rows):
    widths = [(0, 0)] * value.ndim
    widths[-2] = (0, rows - value.shape[-2])
    return jnp.pad(value, widths)


def body(spectra, valid_mask, plan):
    windows = lax.axis_size("window")
    stations, hours, comps, _, bins = spectra.shape
    tiles = bins // LANES
    half = tiles // CORES
    used = hours * comps * half * 2
    rows = -(-used // 32) * 32
    sub = rows // WAYS
    x, z, y, core = coords(lax.axis_index("station"))
    window = lax.axis_index("window")
    basis, turns = tables(bins, hours * windows)

    masked = spectra * valid_mask.astype(jnp.bfloat16)[:, :, None, None, None]
    masked = masked.reshape(stations, hours * comps, 2, tiles, LANES).transpose(0, 1, 3, 2, 4)
    halves = [masked[:, :, n * half:(n + 1) * half].reshape(stations, used, LANES)
              for n in range(CORES)]
    whole = pad_rows(jnp.stack(halves), rows)
    across = pair_permute(whole, 1)
    own = jnp.where(core == 0, whole[0], whole[1])
    other = jnp.where(core == 0, across[0], across[1])
    turns = lax.dynamic_index_in_dim(jnp.asarray(turns), core, 0, keepdims=False)
    right = turn_right(own, other, turns)

    roots = lax.optimization_barrier(jnp.broadcast_to(plan[:, None], (STEPS, LANES)))
    lane = lax.iota(jnp.int32, LANES)
    near = []
    for step in range(STEPS):
        root_x, _, root_y, _ = coords(roots[step])
        near.append((root_x ^ x, root_y ^ y))
    mine = jnp.where(core == 0, roots[0], roots[1])
    first = jnp.where(core == 0, near[0][0], near[1][1])
    second = jnp.where(core == 0, near[0][1], near[1][0])
    _, root_z, _, root_core = coords(mine)
    place = pick(lane, [near[0][0], near[0][1], jnp.broadcast_to(window, (LANES,)),
                        jnp.broadcast_to(core, (LANES,)), near[1][1], near[1][0]])
    block = jnp.where(root_core == core, whole, across)
    parts = [block[:, 0]] + [along_first(block[:, d], d) for d in range(1, WAYS)]
    piece = pick(first, parts)
    cuts = [piece[:, d * sub:(d + 1) * sub] for d in range(WAYS)]
    parts = [cuts[0]] + [along_second(cuts[d], d) for d in range(1, WAYS)]
    small, right = lax.optimization_barrier((pick(second, parts), right))
    small = jnp.where(root_z == z, small, pair_permute(small, 8))
    piece = jnp.concatenate([small] + [along_second(small, d) for d in range(1, WAYS)], 1)
    pieces = [piece] + [along_first(piece, d) for d in range(1, WAYS)]
    own = jnp.stack([jnp.where(core == 0, p[0], p[1]) for p in pieces])
    other = pair_permute(jnp.stack([jnp.where(core == 0, p[1], p[0]) for p in pieces]), 1)
    basis = jnp.asarray(basis)
    kept, given = correlate((1, 2, 3), place, own, other, right, basis)
    total = kept + pair_permute(given, 1)
    place, total = lax.optimization_barrier((place, total))
    parts = [lax.ppermute(total[d - 1], "window", [(w, w ^ d) for w in range(windows)])
             for d in range(1, windows)]
    kept, given = correlate((0,), place, own, other, right, basis)
    given, parts = lax.optimization_barrier((given, parts))
    flip = jnp.asarray(np.eye(HALF, dtype=np.float32)[::-1].copy())
    return finish([kept, pair_permute(given, 1)] + parts, flip).transpose(0, 1, 2, 4, 3, 5)


def solution(mesh):
    return jax.shard_map(
        body,
        mesh=mesh,
        in_specs=(P("station", "window", None, None, None), P("station", "window"), P()),
        out_specs=P("window", None, None, "station", None, None),
        check_vma=False,
    )
```

```python
import functools
import math

import jax
import jax.numpy as jnp
import ml_dtypes
import numpy as np
from jax import lax
from jax.experimental import pallas as pl
from jax.experimental.pallas import tpu as pltpu
from jax.sharding import PartitionSpec as P

LAGS = 512
NW = 18000
STEPS = 2
HALF = LAGS // 2
LANES = 128
CORES = 2
WAYS = 4
DEPTH = 256


def tables(bins, hours):
    freqs = np.arange(bins, dtype=np.int64)[:, None]
    odd = 2 * np.arange(HALF, dtype=np.int64)[None, :] + 1
    angles = ((freqs * odd) % (2 * NW)).astype(np.float64) * (math.pi / NW)
    factor = 1.0 / math.sqrt(2.0 * bins * hours)
    parts = []
    for table in (np.cos(angles) * factor, np.sin(angles) * factor):
        head = table.astype(ml_dtypes.bfloat16)
        tail = (table - head.astype(np.float64)).astype(ml_dtypes.bfloat16)
        parts += [head, tail]
    basis = np.stack(parts, 0).reshape(2, 2, CORES, -1, DEPTH, HALF)
    basis = np.ascontiguousarray(basis.transpose(2, 3, 0, 1, 4, 5))
    turn = np.arange(bins, dtype=np.float64) * (math.pi / NW)
    turns = np.stack([np.cos(turn), np.sin(turn)], 0).astype(np.float32)
    turns = turns.reshape(2, CORES, bins // LANES // CORES, LANES).transpose(1, 2, 0, 3)
    return basis, np.ascontiguousarray(turns)


def coords(index):
    return (index >> 4) & 3, (index >> 3) & 1, (index >> 1) & 3, index & 1


def pair_permute(value, even, odd=None):
    size = lax.axis_size("station")
    shifts = (even, even if odd is None else odd)
    return lax.ppermute(value, "station", [(s, s ^ shifts[s & 1]) for s in range(size)])


def along_first(value, distance):
    return pair_permute(value, distance << 4, distance << 1)


def along_second(value, distance):
    return pair_permute(value, distance << 1, distance << 4)


def swap_window(value, distance):
    size = lax.axis_size("window")
    return lax.ppermute(value, "window", [(w, w ^ distance) for w in range(size)])


def pick(which, values):
    result = values[-1]
    for number in range(len(values) - 2, -1, -1):
        result = jnp.where(which == number, values[number], result)
    return result


def turn_kernel(own, other, turns, out, local):
    rows = own.shape[1]
    tiles = out.shape[0]
    for near, source in enumerate((own, other)):
        for station in range(WAYS):
            at = (near * WAYS + station) * rows
            local[at:at + rows, :] = source[station].astype(jnp.float32)

    def one(tile, carry):
        turn = turns[tile]
        turn_re = jnp.broadcast_to(turn[0:1], (8, LANES))
        turn_im = jnp.broadcast_to(turn[1:2], (8, LANES))
        for part in range(18):
            at = part * 2 * tiles + tile * 2
            x_re = local[pl.ds(at, 8, stride=rows), :]
            x_im = local[pl.ds(at + 1, 8, stride=rows), :]
            out[tile, 2 * part] = x_re * turn_re + x_im * turn_im
            out[tile, 2 * part + 1] = x_im * turn_re - x_re * turn_im
        return carry

    lax.fori_loop(0, tiles, one, 0)


def turn_right(own, other, turns):
    tiles = turns.shape[0]
    rows = own.shape[1]
    return pl.pallas_call(
        turn_kernel,
        in_specs=[pl.BlockSpec(memory_space=pltpu.VMEM)] * 3,
        out_specs=pl.BlockSpec(memory_space=pltpu.VMEM),
        out_shape=jax.ShapeDtypeStruct((tiles, 36, 8, LANES), jnp.float32),
        scratch_shapes=[pltpu.VMEM((8 * rows, LANES), jnp.float32)],
        compiler_params=pltpu.CompilerParams(vmem_limit_bytes=16 * 2**20),
        cost_estimate=pl.CostEstimate(flops=10**7, bytes_accessed=10**6, transcendentals=0),
    )(own, other, turns)


def correlate_kernel(slots, place, own, other, right, basis,
                     mine, theirs, owner, lefts, acc, tables, sems):
    rows = own.shape[1]
    sub = rows // WAYS
    tiles = right.shape[0]
    chunks = tiles * LANES // DEPTH
    window, core = place[2], place[3]
    size = WAYS * rows

    def bring(chunk):
        return pltpu.make_async_copy(basis.at[core, chunk], tables.at[chunk], sems.at[chunk])

    for chunk in range(chunks):
        bring(chunk).start()

    def cross(chunk, slot):
        for part in range(2):
            tile = chunk * 2 + part
            lanes = part * LANES
            turned = [right[tile, n] for n in range(36)]
            sums = [turned[2 * n] + turned[2 * n + 1] for n in range(18)]
            done = []
            for number in range(STEPS * len(slots) * 3):
                step, rest = divmod(number, len(slots) * 3)
                slot_i, comp_i = divmod(rest, 3)
                start = step * size + (window ^ slots[slot_i]) * rows + tile * 2
                parts = [None] * 3
                for hour in range(6):
                    at = start + (hour * 3 + comp_i) * 2 * tiles
                    o_re = jnp.broadcast_to(owner[pl.ds(at, 1), :], (8, LANES))
                    o_im = jnp.broadcast_to(owner[pl.ds(at + 1, 1), :], (8, LANES))
                    o_sum = o_re + o_im
                    o_dif = o_re - o_im
                    for comp in range(3):
                        at = hour * 3 + comp
                        new = (o_re * sums[at], o_sum * turned[2 * at], o_dif * turned[2 * at + 1])
                        parts[comp] = new if hour == 0 else [p + n for p, n in zip(parts[comp], new)]
                done.append(([p[0] - p[2] for p in parts], [p[0] - p[1] for p in parts]))
                if len(done) == 2:
                    where = slice((number - 1) * 24, (number + 1) * 24)
                    for kind in range(2):
                        value = jnp.concatenate(done[0][kind] + done[1][kind], 0)
                        head = value.astype(jnp.bfloat16)
                        tail = (value - head.astype(jnp.float32)).astype(jnp.bfloat16)
                        lefts[slot, kind, where, lanes:lanes + LANES] = head
                        lefts[slot, kind, where, DEPTH + lanes:DEPTH + lanes + LANES] = tail
                    done = []

    def transform(chunk, slot):
        dot = functools.partial(jnp.dot, preferred_element_type=jnp.float32)
        for kind in range(2):
            head = lefts[slot, kind, :, 0:DEPTH]
            tail = lefts[slot, kind, :, DEPTH:2 * DEPTH]
            table = tables[chunk, kind, 0]
            rest = tables[chunk, kind, 1]
            acc[kind] += dot(head, table) + dot(tail, table) + dot(head, rest)

    acc[...] = jnp.zeros_like(acc)
    for step, pieces in ((core, own), (1 - core, other)):
        first, second = place[4 * step], place[4 * step + 1]
        for near in range(WAYS):
            piece = pieces[near].astype(jnp.float32)
            for number in range(WAYS):
                at = pl.multiple_of(step * size + (first ^ near) * rows + (second ^ number) * sub, 8)
                owner[pl.ds(at, sub), :] = piece[number * sub:(number + 1) * sub]
    cross(0, 0)

    def one(chunk, carry):
        slot = lax.rem(chunk, 2)
        bring(chunk).wait()
        transform(chunk, slot)
        cross(chunk + 1, 1 - slot)
        return carry

    lax.fori_loop(0, chunks - 1, one, 0)
    slot = (chunks - 1) % 2
    bring(chunks - 1).wait()
    transform(chunks - 1, slot)
    for kind in range(2):
        lanes = slice(kind * HALF, (kind + 1) * HALF)
        total = acc[kind].reshape(STEPS, len(slots), 9, 8, HALF)
        for step in range(STEPS):
            here = slice(step * 9, step * 9 + 9)
            mine[:, here, :, lanes] = total[step, :, :, 0:4]
            theirs[:, here, :, lanes] = total[step, :, :, 4:8]


def correlate(slots, place, own, other, right, basis):
    rows = own.shape[1]
    chunks = basis.shape[1]
    lines = STEPS * len(slots) * 72
    out = jax.ShapeDtypeStruct((len(slots), STEPS * 9, 4, LAGS), jnp.float32)
    return pl.pallas_call(
        functools.partial(correlate_kernel, slots),
        in_specs=[pl.BlockSpec(memory_space=pltpu.SMEM)]
        + [pl.BlockSpec(memory_space=pltpu.VMEM)] * 3
        + [pl.BlockSpec(memory_space=pl.ANY)],
        out_specs=[pl.BlockSpec(memory_space=pltpu.VMEM)] * 2,
        out_shape=[out, out],
        scratch_shapes=[
            pltpu.VMEM((STEPS * WAYS * rows, LANES), jnp.float32),
            pltpu.VMEM((2, 2, lines, 2 * DEPTH), jnp.bfloat16),
            pltpu.VMEM((2, lines, HALF), jnp.float32),
            pltpu.VMEM(basis.shape[1:], jnp.bfloat16),
            pltpu.SemaphoreType.DMA((chunks,)),
        ],
        compiler_params=pltpu.CompilerParams(vmem_limit_bytes=50 * 2**20),
        cost_estimate=pl.CostEstimate(flops=lines * 3 * 10**7, bytes_accessed=10**6, transcendentals=0),
    )(place, own, other, right, basis)


def finish_kernel(m0, t0, left, left_end, late, late_end, flip, out):
    total = m0[0] + t0[0]
    even = total[:, :, 0:HALF] + (left[0] + left_end[...])
    odd = total[:, :, HALF:LAGS] + (late[0] + late_end[...])
    early = jnp.dot((even + odd).reshape(72, HALF), flip[...], precision=lax.Precision.HIGHEST,
                    preferred_element_type=jnp.float32)
    out[0, :, :, :, :, 0:HALF] = early.reshape(STEPS, 3, 3, 4, HALF)
    out[0, :, :, :, :, HALF:LAGS] = (even - odd).reshape(STEPS, 3, 3, 4, HALF)


def finish(parts, flip):
    return pl.pallas_call(
        finish_kernel,
        out_shape=jax.ShapeDtypeStruct((1, STEPS, 3, 3, 4, LAGS), jnp.float32),
        compiler_params=pltpu.CompilerParams(vmem_limit_bytes=16 * 2**20),
    )(*parts, flip)


def pad_rows(value, rows):
    widths = [(0, 0)] * value.ndim
    widths[-2] = (0, rows - value.shape[-2])
    return jnp.pad(value, widths)


def body(spectra, valid_mask, plan):
    windows = lax.axis_size("window")
    stations, hours, comps, _, bins = spectra.shape
    tiles = bins // LANES
    half = tiles // CORES
    used = hours * comps * half * 2
    rows = -(-used // 32) * 32
    sub = rows // WAYS
    x, z, y, core = coords(lax.axis_index("station"))
    window = lax.axis_index("window")
    basis, turns = tables(bins, hours * windows)

    masked = spectra * valid_mask.astype(jnp.bfloat16)[:, :, None, None, None]
    masked = masked.reshape(stations, hours * comps, 2, tiles, LANES).transpose(0, 1, 3, 2, 4)
    halves = [masked[:, :, n * half:(n + 1) * half].reshape(stations, used, LANES)
              for n in range(CORES)]
    whole = pad_rows(jnp.stack(halves), rows)
    across = pair_permute(whole, 1)
    own = jnp.where(core == 0, whole[0], whole[1])
    other = jnp.where(core == 0, across[0], across[1])
    turns = lax.dynamic_index_in_dim(jnp.asarray(turns), core, 0, keepdims=False)
    right = turn_right(own, other, turns)

    roots = lax.optimization_barrier(jnp.broadcast_to(plan[:, None], (STEPS, LANES)))
    lane = lax.iota(jnp.int32, LANES)
    near = []
    for step in range(STEPS):
        root_x, _, root_y, _ = coords(roots[step])
        near.append((root_x ^ x, root_y ^ y))
    mine = jnp.where(core == 0, roots[0], roots[1])
    first = jnp.where(core == 0, near[0][0], near[1][1])
    second = jnp.where(core == 0, near[0][1], near[1][0])
    _, root_z, _, root_core = coords(mine)
    place = pick(lane, [near[0][0], near[0][1], jnp.broadcast_to(window, (LANES,)),
                        jnp.broadcast_to(core, (LANES,)), near[1][1], near[1][0]])
    block = jnp.where(root_core == core, whole, across)
    parts = [block[:, 0]] + [along_first(block[:, d], d) for d in range(1, WAYS)]
    piece, right = lax.optimization_barrier((pick(first, parts), right))
    cuts = [piece[:, d * sub:(d + 1) * sub] for d in range(WAYS)]
    parts = [cuts[0]] + [along_second(cuts[d], d) for d in range(1, WAYS)]
    small = pick(second, parts)
    small = jnp.where(root_z == z, small, pair_permute(small, 8))
    piece = jnp.concatenate([small] + [along_second(small, d) for d in range(1, WAYS)], 1)
    pieces = [piece] + [along_first(piece, d) for d in range(1, WAYS)]
    own = jnp.stack([jnp.where(core == 0, p[0], p[1]) for p in pieces])
    other = pair_permute(jnp.stack([jnp.where(core == 0, p[1], p[0]) for p in pieces]), 1)
    basis = jnp.asarray(basis)
    kept, given = correlate((1, 2, 3), place, own, other, right, basis)
    total = kept + pair_permute(given, 1)
    place, total = lax.optimization_barrier((place, total))
    left = swap_window(jnp.stack([total[0], total[1]])[..., :HALF], 1)
    late = swap_window(jnp.stack([total[2], total[1]])[..., HALF:], 3)
    kept, given = correlate((0,), place, own, other, right, basis)
    given, left, late = lax.optimization_barrier((given, left, late))
    given = pair_permute(given, 1)
    left_end = swap_window(total[2][..., :HALF] + left[1], 3)
    late_end = swap_window(total[0][..., HALF:] + late[1], 1)
    flip = jnp.asarray(np.eye(HALF, dtype=np.float32)[::-1].copy())
    return finish([kept, given, left, left_end, late, late_end], flip).transpose(0, 1, 2, 4, 3, 5)


def solution(mesh):
    return jax.shard_map(
        body,
        mesh=mesh,
        in_specs=(P("station", "window", None, None, None), P("station", "window"), P()),
        out_specs=P("window", None, None, "station", None, None),
        check_vma=False,
    )
```

```python
import functools
import math

import jax
import jax.numpy as jnp
import ml_dtypes
import numpy as np
from jax import lax
from jax.experimental import pallas as pl
from jax.experimental.pallas import tpu as pltpu
from jax.sharding import PartitionSpec as P

LAGS = 512
NW = 18000
STEPS = 2
HALF = LAGS // 2
LANES = 128
CORES = 2
WAYS = 4
DEPTH = 256


def tables(bins, hours):
    freqs = np.arange(bins, dtype=np.int64)[:, None]
    odd = 2 * np.arange(HALF, dtype=np.int64)[None, :] + 1
    angles = ((freqs * odd) % (2 * NW)).astype(np.float64) * (math.pi / NW)
    factor = 1.0 / math.sqrt(2.0 * bins * hours)
    parts = []
    for table in (np.cos(angles) * factor, np.sin(angles) * factor):
        head = table.astype(ml_dtypes.bfloat16)
        tail = (table - head.astype(np.float64)).astype(ml_dtypes.bfloat16)
        parts += [head, tail]
    basis = np.stack(parts, 0).reshape(2, 2, CORES, -1, DEPTH, HALF)
    basis = np.ascontiguousarray(basis.transpose(2, 3, 0, 1, 4, 5))
    turn = np.arange(bins, dtype=np.float64) * (math.pi / NW)
    turns = np.stack([np.cos(turn), np.sin(turn)], 0).astype(np.float32)
    turns = turns.reshape(2, CORES, bins // LANES // CORES, LANES).transpose(1, 2, 0, 3)
    return basis, np.ascontiguousarray(turns)


def coords(index):
    return (index >> 4) & 3, (index >> 3) & 1, (index >> 1) & 3, index & 1


def pair_permute(value, even, odd=None):
    size = lax.axis_size("station")
    shifts = (even, even if odd is None else odd)
    return lax.ppermute(value, "station", [(s, s ^ shifts[s & 1]) for s in range(size)])


def along_first(value, distance):
    return pair_permute(value, distance << 4, distance << 1)


def along_second(value, distance):
    return pair_permute(value, distance << 1, distance << 4)


def swap_window(value, distance):
    size = lax.axis_size("window")
    return lax.ppermute(value, "window", [(w, w ^ distance) for w in range(size)])


def pick(which, values):
    result = values[-1]
    for number in range(len(values) - 2, -1, -1):
        result = jnp.where(which == number, values[number], result)
    return result


def turn_kernel(own, other, turns, out, local):
    rows = own.shape[1]
    tiles = out.shape[0]
    for near, source in enumerate((own, other)):
        for station in range(WAYS):
            at = (near * WAYS + station) * rows
            local[at:at + rows, :] = source[station].astype(jnp.float32)

    def one(tile, carry):
        turn = turns[tile]
        turn_re = jnp.broadcast_to(turn[0:1], (8, LANES))
        turn_im = jnp.broadcast_to(turn[1:2], (8, LANES))
        for part in range(18):
            at = part * 2 * tiles + tile * 2
            x_re = local[pl.ds(at, 8, stride=rows), :]
            x_im = local[pl.ds(at + 1, 8, stride=rows), :]
            out[tile, 2 * part] = x_re * turn_re + x_im * turn_im
            out[tile, 2 * part + 1] = x_im * turn_re - x_re * turn_im
        return carry

    lax.fori_loop(0, tiles, one, 0)


def turn_right(own, other, turns):
    tiles = turns.shape[0]
    rows = own.shape[1]
    return pl.pallas_call(
        turn_kernel,
        in_specs=[pl.BlockSpec(memory_space=pltpu.VMEM)] * 3,
        out_specs=pl.BlockSpec(memory_space=pltpu.VMEM),
        out_shape=jax.ShapeDtypeStruct((tiles, 36, 8, LANES), jnp.float32),
        scratch_shapes=[pltpu.VMEM((8 * rows, LANES), jnp.float32)],
        compiler_params=pltpu.CompilerParams(vmem_limit_bytes=16 * 2**20),
        cost_estimate=pl.CostEstimate(flops=10**7, bytes_accessed=10**6, transcendentals=0),
    )(own, other, turns)


def correlate_kernel(slots, place, own, other, right, basis,
                     mine, theirs, owner, lefts, acc, tables, sems):
    rows = own.shape[1]
    sub = rows // WAYS
    tiles = right.shape[0]
    chunks = tiles * LANES // DEPTH
    window, core = place[2], place[3]
    size = WAYS * rows

    def bring(chunk):
        return pltpu.make_async_copy(basis.at[core, chunk], tables.at[chunk], sems.at[chunk])

    for chunk in range(chunks):
        bring(chunk).start()

    def cross(chunk, slot):
        for part in range(2):
            tile = chunk * 2 + part
            lanes = part * LANES
            turned = [right[tile, n] for n in range(36)]
            sums = [turned[2 * n] + turned[2 * n + 1] for n in range(18)]
            done = []
            for number in range(STEPS * len(slots) * 3):
                step, rest = divmod(number, len(slots) * 3)
                slot_i, comp_i = divmod(rest, 3)
                start = step * size + (window ^ slots[slot_i]) * rows + tile * 2
                parts = [None] * 3
                for hour in range(6):
                    at = start + (hour * 3 + comp_i) * 2 * tiles
                    o_re = jnp.broadcast_to(owner[pl.ds(at, 1), :], (8, LANES))
                    o_im = jnp.broadcast_to(owner[pl.ds(at + 1, 1), :], (8, LANES))
                    o_sum = o_re + o_im
                    o_dif = o_re - o_im
                    for comp in range(3):
                        at = hour * 3 + comp
                        new = (o_re * sums[at], o_sum * turned[2 * at], o_dif * turned[2 * at + 1])
                        parts[comp] = new if hour == 0 else [p + n for p, n in zip(parts[comp], new)]
                done.append(([p[0] - p[2] for p in parts], [p[0] - p[1] for p in parts]))
                if len(done) == 2:
                    where = slice((number - 1) * 24, (number + 1) * 24)
                    for kind in range(2):
                        value = jnp.concatenate(done[0][kind] + done[1][kind], 0)
                        head = value.astype(jnp.bfloat16)
                        tail = (value - head.astype(jnp.float32)).astype(jnp.bfloat16)
                        lefts[slot, kind, where, lanes:lanes + LANES] = head
                        lefts[slot, kind, where, DEPTH + lanes:DEPTH + lanes + LANES] = tail
                    done = []

    def transform(chunk, slot):
        dot = functools.partial(jnp.dot, preferred_element_type=jnp.float32)
        for kind in range(2):
            head = lefts[slot, kind, :, 0:DEPTH]
            tail = lefts[slot, kind, :, DEPTH:2 * DEPTH]
            table = tables[chunk, kind, 0]
            rest = tables[chunk, kind, 1]
            acc[kind] += dot(head, table) + dot(tail, table) + dot(head, rest)

    acc[...] = jnp.zeros_like(acc)
    for step, pieces in ((core, own), (1 - core, other)):
        first, second = place[4 * step], place[4 * step + 1]
        for used in slots:
            piece = pieces[first ^ window ^ used].astype(jnp.float32)
            for number in range(WAYS):
                at = pl.multiple_of(step * size + (window ^ used) * rows + (second ^ number) * sub, 8)
                owner[pl.ds(at, sub), :] = piece[number * sub:(number + 1) * sub]
    cross(0, 0)

    def one(chunk, carry):
        slot = lax.rem(chunk, 2)
        bring(chunk).wait()
        transform(chunk, slot)
        cross(chunk + 1, 1 - slot)
        return carry

    lax.fori_loop(0, chunks - 1, one, 0)
    slot = (chunks - 1) % 2
    bring(chunks - 1).wait()
    transform(chunks - 1, slot)
    for kind in range(2):
        lanes = slice(kind * HALF, (kind + 1) * HALF)
        total = acc[kind].reshape(STEPS, len(slots), 9, 8, HALF)
        for step in range(STEPS):
            here = slice(step * 9, step * 9 + 9)
            mine[:, here, :, lanes] = total[step, :, :, 0:4]
            theirs[:, here, :, lanes] = total[step, :, :, 4:8]


def correlate(slots, place, own, other, right, basis):
    rows = own.shape[1]
    chunks = basis.shape[1]
    lines = STEPS * len(slots) * 72
    out = jax.ShapeDtypeStruct((len(slots), STEPS * 9, 4, LAGS), jnp.float32)
    return pl.pallas_call(
        functools.partial(correlate_kernel, slots),
        in_specs=[pl.BlockSpec(memory_space=pltpu.SMEM)]
        + [pl.BlockSpec(memory_space=pltpu.VMEM)] * 3
        + [pl.BlockSpec(memory_space=pl.ANY)],
        out_specs=[pl.BlockSpec(memory_space=pltpu.VMEM)] * 2,
        out_shape=[out, out],
        scratch_shapes=[
            pltpu.VMEM((STEPS * WAYS * rows, LANES), jnp.float32),
            pltpu.VMEM((2, 2, lines, 2 * DEPTH), jnp.bfloat16),
            pltpu.VMEM((2, lines, HALF), jnp.float32),
            pltpu.VMEM(basis.shape[1:], jnp.bfloat16),
            pltpu.SemaphoreType.DMA((chunks,)),
        ],
        compiler_params=pltpu.CompilerParams(vmem_limit_bytes=50 * 2**20),
        cost_estimate=pl.CostEstimate(flops=lines * 3 * 10**7, bytes_accessed=10**6, transcendentals=0),
    )(place, own, other, right, basis)


def finish_kernel(m0, t0, left, left_end, late, late_end, flip, out):
    total = m0[0] + t0[0]
    even = total[:, :, 0:HALF] + (left[0] + left_end[...])
    odd = total[:, :, HALF:LAGS] + (late[0] + late_end[...])
    early = jnp.dot((even + odd).reshape(72, HALF), flip[...], precision=lax.Precision.HIGHEST,
                    preferred_element_type=jnp.float32)
    out[0, :, :, :, :, 0:HALF] = early.reshape(STEPS, 3, 3, 4, HALF)
    out[0, :, :, :, :, HALF:LAGS] = (even - odd).reshape(STEPS, 3, 3, 4, HALF)


def finish(parts, flip):
    return pl.pallas_call(
        finish_kernel,
        out_shape=jax.ShapeDtypeStruct((1, STEPS, 3, 3, 4, LAGS), jnp.float32),
        compiler_params=pltpu.CompilerParams(vmem_limit_bytes=16 * 2**20),
    )(*parts, flip)


def pad_rows(value, rows):
    widths = [(0, 0)] * value.ndim
    widths[-2] = (0, rows - value.shape[-2])
    return jnp.pad(value, widths)


def body(spectra, valid_mask, plan):
    windows = lax.axis_size("window")
    stations, hours, comps, _, bins = spectra.shape
    tiles = bins // LANES
    half = tiles // CORES
    used = hours * comps * half * 2
    rows = -(-used // 32) * 32
    sub = rows // WAYS
    x, z, y, core = coords(lax.axis_index("station"))
    window = lax.axis_index("window")
    basis, turns = tables(bins, hours * windows)

    masked = spectra * valid_mask.astype(jnp.bfloat16)[:, :, None, None, None]
    masked = masked.reshape(stations, hours * comps, 2, tiles, LANES).transpose(0, 1, 3, 2, 4)
    halves = [masked[:, :, n * half:(n + 1) * half].reshape(stations, used, LANES)
              for n in range(CORES)]
    rest = pad_rows(jnp.stack([h[1:] for h in halves]), rows)
    lead = pad_rows(jnp.stack([h[0] for h in halves]), rows)
    far_rest = pair_permute(rest, 1)
    own = pad_rows(jnp.where(core == 0, halves[0], halves[1]), rows)
    turns = lax.dynamic_index_in_dim(jnp.asarray(turns), core, 0, keepdims=False)

    roots = lax.optimization_barrier(jnp.broadcast_to(plan[:, None], (STEPS, LANES)))
    lane = lax.iota(jnp.int32, LANES)
    near = []
    for step in range(STEPS):
        root_x, _, root_y, _ = coords(roots[step])
        near.append((root_x ^ x, root_y ^ y))
    mine = jnp.where(core == 0, roots[0], roots[1])
    first = jnp.where(core == 0, near[0][0], near[1][1])
    second = jnp.where(core == 0, near[0][1], near[1][0])
    _, root_z, _, root_core = coords(mine)
    place = pick(lane, [near[0][0], near[0][1], jnp.broadcast_to(window, (LANES,)),
                        jnp.broadcast_to(core, (LANES,)), near[1][1], near[1][0]])
    block = jnp.where(root_core == core, rest, far_rest)
    parts = [along_first(block[:, d - 1], d) for d in range(1, WAYS)]
    far_lead = pair_permute(lead, 1)
    parts = [jnp.where(root_core == core, lead, far_lead)] + parts
    other = jnp.concatenate([jnp.where(core == 0, far_lead[0], far_lead[1])[None],
                             jnp.where(core == 0, far_rest[0], far_rest[1])], 0)
    right = turn_right(own, other, turns)
    piece, right = lax.optimization_barrier((pick(first, parts), right))
    cuts = [piece[:, d * sub:(d + 1) * sub] for d in range(WAYS)]
    parts = [cuts[0]] + [along_second(cuts[d], d) for d in range(1, WAYS)]
    small = pick(second, parts)
    small = jnp.where(root_z == z, small, pair_permute(small, 8))
    piece = jnp.concatenate([small] + [along_second(small, d) for d in range(1, WAYS)], 1)
    pieces = [piece] + [along_first(piece, d) for d in range(1, WAYS)]
    own = jnp.stack([jnp.where(core == 0, p[0], p[1]) for p in pieces])
    other = pair_permute(jnp.stack([jnp.where(core == 0, p[1], p[0]) for p in pieces]), 1)
    basis = jnp.asarray(basis)
    kept, given = correlate((1, 2, 3), place, own, other, right, basis)
    total = kept + pair_permute(given, 1)
    place, total = lax.optimization_barrier((place, total))
    left = swap_window(jnp.stack([total[0], total[1]])[..., :HALF], 1)
    late = swap_window(jnp.stack([total[2], total[1]])[..., HALF:], 3)
    kept, given = correlate((0,), place, own, other, right, basis)
    given, left, late = lax.optimization_barrier((given, left, late))
    given = pair_permute(given, 1)
    left_end = swap_window(total[2][..., :HALF] + left[1], 3)
    late_end = swap_window(total[0][..., HALF:] + late[1], 1)
    flip = jnp.asarray(np.eye(HALF, dtype=np.float32)[::-1].copy())
    return finish([kept, given, left, left_end, late, late_end], flip).transpose(0, 1, 2, 4, 3, 5)


def solution(mesh):
    return jax.shard_map(
        body,
        mesh=mesh,
        in_specs=(P("station", "window", None, None, None), P("station", "window"), P()),
        out_specs=P("window", None, None, "station", None, None),
        check_vma=False,
    )
```
